32 devices in a mesh: leaf: 8 (over y, x, core), probe: 4 (over z).
Axes of the slice: x: 2, y: 2, z: 4, core: 2. Of those that a mesh axis runs over, the one named last changes fastest.
Arguments:
- points: bfloat16 [32768, 2048], P('leaf', 'probe'), parts along dimension 1, may hold values from -6 to 6
- leaf_basis: bfloat16 [128, 64, 256], P('leaf'), may hold values from -0.375 to 0.375
- local_transfer: bfloat16 [240, 4096], P('leaf'), may hold values from -0.5 to 0.5
- top_transfer: bfloat16 [14, 4096], replicated, may hold values from -0.5 to 0.5
- sources: int32 [8184], P('leaf'), may hold values from 0 to 127, as said below
- couplings: bfloat16 [8184, 4096], P('leaf'), as said below
Outputs:
- coupled: bfloat16 [248, 64, 2048], P('leaf', None, 'probe'), parts along dimension 2
- ancestors: bfloat16 [8, 3, 64, 2048], P('leaf', None, None, 'probe'), parts along dimension 3
The draws below stay inside these ranges and needn't reach their ends.
There are 4 independent parts, one for each index of `probe`. The reference program is written for one: setup_inputs(seed, part) draws one part's arguments, and reference() takes and returns one part's arrays. A program takes and returns all parts, laid end to end along the dimension named above; an argument that names none is the same for every part. Nothing has to cross between parts.
Inputs may be any that keep to these rules, and one draw needn't show every extreme that they name: `sources`: each entry names a cluster of its target's level lying in the target's subtree or in one of the two subtrees on either side; the entries of one target are distinct. `couplings`: tiles of level h have entries of deviation (3 * 64 * 16 / 2^h)^(-1/2).
All inputs are finite; a program needn't handle non-finite values.
Results may differ from the reference program's by a relative error of at most 0.0095.
Values may be sent and summed in bfloat16 or wider, within the bound.
A program may use at most 128 MiB of HBM per device.

```python
from functools import partial
import jax
import jax.numpy as jnp
from jax import lax

LEAF = 256
RANK = 64
PROBES = 512
LOCAL = 5
TOP = 3
LEAF_DEV = 16
NLEAF = 128
POINTS = 32768
TARGETS_DEV = 31
LINKS_DEV = 30
PAIRS_DEV = 1023
TOP_LINKS = 14
N_LEAF = 8


def draw_sources(key, part):
    pieces = []
    for height in range(LOCAL):
        number = LEAF_DEV >> height
        breadth = 5 * number
        clusters = number * N_LEAF
        scores = jax.random.randint(jax.random.fold_in(key, height), (N_LEAF, number, breadth), 0, 2 ** 20)
        columns = jnp.arange(breadth, dtype=jnp.int32)
        anchor = (jnp.arange(N_LEAF, dtype=jnp.int32) - 2) * number
        candidates = anchor[:, None, None] + columns[None, None, :]
        inside = (candidates >= 0) & (candidates < clusters)
        ranked_keys = scores * (8 * number) + columns + jnp.where(inside, 0, 2 ** 29)
        ranked = jnp.argsort(ranked_keys, axis=-1)[:, :, :3 * number]
        chosen = jnp.take_along_axis(candidates, ranked, axis=-1)
        pieces.append(chosen.reshape(N_LEAF, 3 * number * number))
    return jnp.concatenate(pieces, axis=1).reshape(N_LEAF * PAIRS_DEV).astype(jnp.int32)


def draw_couplings(key, part):
    pieces = []
    for height in range(LOCAL):
        number = LEAF_DEV >> height
        spread = (3.0 * RANK * number) ** (-0.5)
        extent = (N_LEAF, 3 * number * number, RANK * RANK)
        level_key = jax.random.fold_in(key, 100 + height)
        values = jax.random.normal(level_key, extent, jnp.float32)
        pieces.append(values * spread)
    return jnp.concatenate(pieces, axis=1).reshape(N_LEAF * PAIRS_DEV, RANK * RANK).astype(jnp.bfloat16)


def shard_levels(stream_key, shape, cuts, least, top_value):
    factor_of, own = 1.0, jax.random.fold_in(stream_key, 6)
    for axis_at, shards_of in cuts:
        heights = jnp.exp(jax.random.uniform(jax.random.fold_in(own, axis_at), (shards_of,), jnp.float32, least / len(cuts), top_value / len(cuts)))
        factor_of = factor_of * jnp.repeat(heights, shape[axis_at] // shards_of).reshape([-1 if axis == axis_at else 1 for axis in range(len(shape))])
    return factor_of


def normal_values(stream_key, dims, scale, bound, cuts=(), held_as=jnp.bfloat16):
    level = shard_levels(stream_key, dims, cuts, -0.22, 0.18) if cuts else 1.0
    values = jax.random.normal(stream_key, dims, jnp.float32) * scale * level
    return jnp.minimum(jnp.maximum(values, -bound), bound).astype(held_as)


def setup_inputs(seed: int = 0, part: int = 0) -> dict:
    keys = jax.random.split(jax.random.key(seed), 7)
    own_keys = jax.random.split(jax.random.fold_in(keys[6], part), 7)
    return {
        "points": normal_values(own_keys[0], (POINTS, PROBES), 1.0, 6.0, ((0, 8),)),
        "leaf_basis": normal_values(keys[1], (NLEAF, RANK, LEAF), LEAF ** -0.5, 0.375, ((0, 8),)),
        "local_transfer": normal_values(keys[2], (LINKS_DEV * N_LEAF, RANK * RANK), (2 * RANK) ** -0.5, 0.5, ((0, 8),)),
        "top_transfer": normal_values(keys[3], (TOP_LINKS, RANK * RANK), (2 * RANK) ** -0.5, 0.5),
        "sources": draw_sources(jax.random.fold_in(keys[6], 71), part),
        "couplings": draw_couplings(jax.random.fold_in(keys[6], 71), part),
    }


def lift_level(children, matrices):
    products = jnp.einsum("cab,cap->cbp", matrices.astype(jnp.float32).reshape(-1, RANK, RANK), children.astype(jnp.float32), precision=lax.Precision.HIGHEST)
    return products.reshape(-1, 2, RANK, PROBES).sum(axis=1)


def couple_block(operands, level_moments, number):
    block_sources, block_tiles = operands
    picked = jnp.take(level_moments, block_sources, axis=0).astype(jnp.float32).reshape(number, 3 * number, RANK, PROBES)
    matrices = block_tiles.astype(jnp.float32).reshape(number, 3 * number, RANK, RANK)
    summed = jnp.einsum("tkab,tkap->tbp", matrices, picked, precision=lax.Precision.HIGHEST)
    return summed.astype(jnp.bfloat16)


def reference(points, leaf_basis, local_transfer, top_transfer, sources, couplings):
    blocks = points.reshape(NLEAF, LEAF, PROBES).astype(jnp.float32)
    first = jnp.einsum("jrl,jlp->jrp", leaf_basis.astype(jnp.float32), blocks, precision=lax.Precision.HIGHEST)
    moments = [first.astype(jnp.bfloat16)]
    link_rows = local_transfer.reshape(N_LEAF, LINKS_DEV, RANK * RANK)
    cursor = 0
    for height in range(1, LOCAL):
        number = LEAF_DEV >> (height - 1)
        matrices = link_rows[:, cursor:cursor + number].reshape(N_LEAF * number, RANK * RANK)
        moments.append(lift_level(moments[-1], matrices).astype(jnp.bfloat16))
        cursor += number
    source_rows = sources.reshape(N_LEAF, PAIRS_DEV)
    tile_rows = couplings.reshape(N_LEAF, PAIRS_DEV, RANK * RANK)
    outputs = []
    cursor = 0
    for height in range(LOCAL):
        number = LEAF_DEV >> height
        entries = 3 * number * number
        worker = partial(couple_block, level_moments=moments[height], number=number)
        outputs.append(lax.map(worker, (source_rows[:, cursor:cursor + entries], tile_rows[:, cursor:cursor + entries])))
        cursor += entries
    coupled = jnp.concatenate(outputs, axis=1).reshape(N_LEAF * TARGETS_DEV, RANK, PROBES)
    current = moments[LOCAL - 1]
    ladder = []
    cursor = 0
    for height in range(TOP):
        clusters = current.shape[0]
        current = lift_level(current, top_transfer[cursor:cursor + clusters]).astype(jnp.bfloat16)
        cursor += clusters
        ladder.append(jnp.repeat(current, 2 ** (height + 1), axis=0))
    ancestors = jnp.stack(ladder, axis=1)
    return coupled, ancestors
```

```python
import functools

import jax
import jax.numpy as jnp
from jax import lax
from jax.experimental import pallas as pl
from jax.experimental.pallas import tpu as pltpu
from jax.sharding import PartitionSpec as P

RANK = 64
CHUNKS = 4
BF = jnp.bfloat16
F32 = jnp.float32


def matmul(a, b):
    return lax.dot_general(a, b, (((1,), (0,)), ((), ())), preferred_element_type=F32)


def matmul_t(a, b):
    return lax.dot_general(a, b, (((0,), (0,)), ((), ())), preferred_element_type=F32)


class Route:
    def __init__(self, sends, target, takes, origin, after):
        self.sends = sends
        self.target = target
        self.takes = takes
        self.origin = origin
        self.after = after


def routes_of(n, me):
    def among(*devices):
        found = me == devices[0]
        for device in devices[1:]:
            found = found | (me == device)
        return found

    if n == 8:
        flip = [me + 1 - 2 * (me % 2), me + 2 - 4 * ((me // 2) % 2), me + 4 - 8 * (me // 4)]
        other = 7 - me
        always = me >= 0
        cross3 = flip[1] + 1 - 2 * (flip[1] % 2)
        cross6 = flip[1] + 4 - 8 * (flip[1] // 4)
        return [
            Route(always, flip[0], always, flip[0], None),
            Route(always, flip[1], always, flip[1], None),
            Route(among(0, 3, 4, 7), flip[0], among(1, 2, 5, 6), cross3, 1),
            Route(among(0, 1, 6, 7), flip[2], among(2, 3, 4, 5), cross6, 1),
            Route(among(2, 5), flip[0], among(3, 4), other, 3),
        ]
    return [
        Route((me + o >= 0) & (me + o < n), me + o, (me - o >= 0) & (me - o < n), me - o, None)
        for o in (1, -1, 2, -2)
    ]


def kernel(n, leaves, probes, points, basis, lifts, tops, keys, couplings, coupled, ancestors,
           pts, tiles, own, got, got_lifts, lifted, spread, w0, w1, wu, acc, ladder,
           pts_sem, tile_sem, send_sem, recv_sem, up_send, up_recv):
    me = lax.axis_index("leaf")
    ups = n.bit_length() - 1
    leaf = pts.shape[0] // leaves
    per = leaves // CHUNKS
    routes = routes_of(n, me)
    partners = []
    for h in range(ups):
        bit = (me // (1 << h)) % 2
        partners.append((bit, me + (1 << h) * (1 - 2 * bit)))

    def point_copy(k):
        rows = pl.ds(k * per * leaf, per * leaf)
        return pltpu.make_async_copy(points.at[rows, :], pts.at[rows, :], pts_sem.at[k])

    tile_copy = pltpu.make_async_copy(couplings, tiles, tile_sem)
    for k in range(CHUNKS):
        point_copy(k).start()
    tile_copy.start()

    barrier = pltpu.get_barrier_semaphore()
    greeted = [(None, device) for _, device in partners]
    if n != 8:
        greeted += [(r.sends, r.target) for r in routes]
    for valid, device in greeted:
        def greet(device=device):
            pl.semaphore_signal(barrier, inc=1, device_id={"leaf": device},
                                device_id_type=pl.DeviceIdType.MESH)
        greet() if valid is None else pl.when(valid)(greet)
    expected = ups
    if n != 8:
        expected += sum(r.takes.astype(jnp.int32) for r in routes)
    pl.semaphore_wait(barrier, expected)

    def move(i, k):
        route = routes[i]
        if k == CHUNKS:
            src = lifts if route.after is None else got_lifts.at[route.after]
            dst = got_lifts.at[i]
        else:
            rows = pl.ds(k * per * RANK, per * RANK)
            src = own.at[rows, :] if route.after is None else got.at[route.after, rows, :]
            dst = got.at[i, rows, :]
        return pltpu.make_async_remote_copy(
            src_ref=src, dst_ref=dst, send_sem=send_sem.at[i, k], recv_sem=recv_sem.at[i, k],
            device_id={"leaf": route.target}, device_id_type=pl.DeviceIdType.MESH)

    def send(i, k):
        pl.when(routes[i].sends)(lambda: move(i, k).start())

    arrived = set()

    def arrive(i, k):
        if (i, k) in arrived:
            return
        arrived.add((i, k))
        pl.when(routes[i].takes)(lambda: move(i, k).wait_recv())
        for later, route in enumerate(routes):
            if route.after == i:
                send(later, k)

    for i, route in enumerate(routes):
        if route.after is None:
            send(i, CHUNKS)

    for k in range(CHUNKS):
        point_copy(k).wait()
        for j in range(k * per, (k + 1) * per):
            own[j * RANK:(j + 1) * RANK, :] = matmul(
                basis[j], pts[j * leaf:(j + 1) * leaf, :]).astype(BF)
        for i, route in enumerate(routes):
            if route.after is None:
                send(i, k)

    def lift_all(source, matrices):
        half = leaves // 2
        for i in range(leaves - 1):
            if i < half:
                pair = source[2 * i * RANK:(2 * i + 2) * RANK, :]
            else:
                at = 2 * (i - half)
                pair = lifted[at * RANK:(at + 2) * RANK, :]
            lifted[i * RANK:(i + 1) * RANK, :] = matmul(
                matrices[i * RANK:(i + 1) * RANK, :], pair).astype(BF)

    def climb(h):
        bit, device = partners[h]
        return pltpu.make_async_remote_copy(
            src_ref=ladder.at[h, bit], dst_ref=ladder.at[h, bit], send_sem=up_send.at[h],
            recv_sem=up_recv.at[h], device_id={"leaf": device}, device_id_type=pl.DeviceIdType.MESH)

    def climb_end(h):
        climb(h).wait_recv()
        pairs = sum(n >> (g + 1) for g in range(h))
        row = (pairs + me // (1 << (h + 1))) * RANK
        matrix = tops[pl.ds(pl.multiple_of(row, RANK), RANK), :]
        both = ladder[h].reshape(2 * RANK, probes)
        value = matmul(matrix, both).astype(BF)
        ancestors[0, h] = value
        if h + 1 < ups:
            ladder[h + 1, partners[h + 1][0]] = value
            climb(h + 1).start()

    lift_all(own, lifts)
    ladder[0, partners[0][0]] = lifted[(leaves - 2) * RANK:(leaves - 1) * RANK, :]
    climb(0).start()

    tile_copy.wait()
    wide = 512

    def two_sides(block, first_half):
        block = block.astype(F32)
        rolled = jnp.concatenate(
            [pltpu.roll(block[:, g * 128:(g + 1) * 128], 64, 1) for g in range(wide // 128)], axis=1)
        lane = lax.broadcasted_iota(jnp.int32, block.shape, 1) % 128 < 64
        keep = lane == first_half
        even = jnp.where(keep, jnp.where(first_half, block, rolled), 0.0)
        odd = jnp.where(keep, jnp.where(first_half, rolled, block), 0.0)
        return even.astype(BF), odd.astype(BF)

    def one_hot(row, count, entries, allowed=None):
        slots = lax.broadcasted_iota(jnp.int32, (count, entries), 0)
        hit = slots == keys[row:row + 1, :entries] if isinstance(row, int) else (
            slots == keys[pl.ds(row, 1), :][:, :entries])
        if allowed is not None:
            hit = hit & allowed
        return jnp.where(hit, 1.0, 0.0).astype(BF)

    def put(evens, odds, base, ref_of, group, lanes):
        both = jnp.concatenate([evens[base:base + 8], odds[base:base + 8]], axis=0).astype(BF)
        for q in range(wide // 128):
            at = (group * (wide // 128) + q) * 16
            ref_of[at:at + 16, lanes] = both[:, q * 128:(q + 1) * 128]

    groups = RANK * RANK // wide
    e0, e1 = 6 * leaves, 3 * leaves

    def place0(j):
        rows = pl.ds(pl.multiple_of(j * e0, 32), e0)
        lanes = pl.ds(pl.multiple_of(j * 128, 128), 128)
        first = lax.broadcasted_iota(jnp.int32, (e0, wide), 0) < e0 // 2
        hot = one_hot(j, 5 * leaves, e0)
        for g in range(groups):
            even, odd = two_sides(tiles[rows, g * wide:(g + 1) * wide], first)
            evens, odds = matmul(hot, even), matmul(hot, odd)
            for d in range(5):
                for half in range(2):
                    put(evens, odds, d * leaves + half * 8, w0.at[d, half], g, lanes)

    def place1(j):
        rows = pl.ds(pl.multiple_of(leaves * e1 + j * e1, 16), e1)
        lanes = pl.ds(pl.multiple_of(j * 128, 128), 128)
        first = lax.broadcasted_iota(jnp.int32, (e1, wide), 0) < e1 // 2
        hot = one_hot(leaves // 2 + j, 5 * 8, e1)
        for g in range(groups):
            even, odd = two_sides(tiles[rows, g * wide:(g + 1) * wide], first)
            evens, odds = matmul(hot, even), matmul(hot, odd)
            for d in range(5):
                put(evens, odds, d * 8, w1.at[d], g, lanes)

    def place_upper():
        start = leaves * e1 + (leaves // 2) * (e1 // 2)
        count = tiles.shape[0] - start
        row = lax.broadcasted_iota(jnp.int32, (count, wide), 0)
        first = (row < 12) | ((row >= 24) & (row < 36)) | ((row >= 48) & (row < 54)) | (row >= 60)
        entry = lax.broadcasted_iota(jnp.int32, (40, count), 1)
        hots = []
        for low, high in ((0, 24), (24, 48), (48, 60), (60, 63)):
            hots.append(one_hot(3 * leaves // 4, 40, count, (entry >= low) & (entry < high)))
        hot = jnp.concatenate(hots, axis=0)
        for g in range(groups):
            even, odd = two_sides(tiles[start:, g * wide:(g + 1) * wide], first)
            evens, odds = matmul(hot, even), matmul(hot, odd)
            for j in range(4):
                for d in range(5):
                    put(evens, odds, j * 40 + d * 8, wu.at[d], g, slice(j * 128, (j + 1) * 128))

    def spread_rows(source, first, blocks):
        for s, block in enumerate(blocks):
            at = (first + block) * RANK
            rows = source[at:at + RANK, :].astype(F32)
            for c in range(probes // 128):
                spread[c, pl.ds(s, RANK, stride=8), :] = rows[:, c * 128:(c + 1) * 128]
        return jnp.concatenate([spread[c].astype(BF) for c in range(probes // 128)], axis=1)

    def add_in(weights, columns, base, moments, fresh):
        @pl.loop(0, columns // 256)
        def _(c):
            at = pl.multiple_of(c * 256, 256)
            part = matmul_t(weights[:, pl.ds(at, 256)], moments)
            rows = pl.ds(pl.multiple_of(base + at, 256), 256)
            if fresh:
                acc[rows, :] = part
            else:
                acc[rows, :] += part

    def couple(source, matrices, d, fresh=False, lift=True):
        if lift:
            lift_all(source, matrices)
        width = leaves * RANK
        add_in(w0.at[d, 0], width, 0, spread_rows(source, 0, range(8)), fresh)
        add_in(w0.at[d, 1], width, 0, spread_rows(source, 8, range(8)), False)
        add_in(w1.at[d], width // 2, width, spread_rows(lifted, 0, range(8)), fresh)
        add_in(wu.at[d], width // 2, width + width // 2,
               spread_rows(lifted, 8, (0, 1, 2, 3, 4, 5, 6, 6)), fresh)

    passed_on = sorted({r.after for r in routes if r.after is not None})
    for i in passed_on:
        arrive(i, CHUNKS)
    for step in range(4):
        @pl.loop(2 * step, 2 * step + 2)
        def _(j):
            place0(j)
        if step < CHUNKS - 1:
            for i in passed_on:
                arrive(i, step)
        if step < ups:
            climb_end(step)
    for h in range(4, ups):
        climb_end(h)
    pl.loop(0, leaves // 4)(place1)
    place_upper()
    for i in passed_on:
        arrive(i, CHUNKS - 1)
    couple(own, lifts, 2, fresh=True, lift=False)
    for i, route in enumerate(routes):
        for k in range(CHUNKS + 1):
            arrive(i, k)

        @pl.when(route.takes)
        def _():
            couple(got.at[i], got_lifts.at[i], route.origin - me + 2)

    for t in range(2 * leaves - 1):
        coupled[t] = acc[t * RANK:(t + 1) * RANK, :].astype(BF)

    for i, route in enumerate(routes):
        for k in range(CHUNKS + 1):
            pl.when(route.sends)(lambda i=i, k=k: move(i, k).wait_send())
    for h in range(ups):
        climb(h).wait_send()


def side_by_side(matrices):
    pairs = matrices.reshape(-1, 2, RANK, RANK).transpose(0, 3, 1, 2)
    return pairs.reshape(-1, 2 * RANK)


def source_keys(sources, device, leaves):
    rows, cursor = [], 0
    upper = []
    for height in range(leaves.bit_length()):
        number = leaves >> height
        entries = 3 * number * number
        local = sources[cursor:cursor + entries] - (device - 2) * number
        cursor += entries
        if height < 2:
            local = local.reshape(number // 2, 6 * number)
            rows.append(jnp.pad(local, ((0, 0), (0, 128 - 6 * number)), constant_values=-1))
        else:
            shift = 8 - 2 * number
            upper.append(local // number * 8 + local % number + shift)
    last = jnp.concatenate(upper)
    rows.append(jnp.pad(last, (0, 128 - last.shape[0]), constant_values=-1)[None])
    rows.append(jnp.full((3, 128), -1, jnp.int32))
    return jnp.concatenate(rows, axis=0)


def shards(points, leaf_basis, local_transfer, top_transfer, sources, couplings):
    n = lax.axis_size("leaf")
    leaves, _, leaf = leaf_basis.shape
    probes = points.shape[1]
    ups = n.bit_length() - 1
    keys = source_keys(sources, lax.axis_index("leaf"), leaves)
    block = leaves * RANK
    count = 5 if n == 8 else 4
    vmem = pl.BlockSpec(memory_space=pltpu.VMEM)
    anywhere = pl.BlockSpec(memory_space=pl.ANY)
    return pl.pallas_call(
        functools.partial(kernel, n, leaves, probes),
        out_shape=(
            jax.ShapeDtypeStruct((2 * leaves - 1, RANK, probes), BF),
            jax.ShapeDtypeStruct((1, ups, RANK, probes), BF),
        ),
        in_specs=[anywhere, vmem, vmem, vmem, vmem, anywhere],
        out_specs=(vmem, vmem),
        scratch_shapes=[
            pltpu.VMEM(points.shape, BF),
            pltpu.VMEM(couplings.shape, BF),
            pltpu.VMEM((block, probes), BF),
            pltpu.VMEM((count, block, probes), BF),
            pltpu.VMEM((count, block - RANK, 2 * RANK), BF),
            pltpu.VMEM((block - RANK, probes), BF),
            pltpu.VMEM((probes // 128, 8 * RANK, 128), F32),
            pltpu.VMEM((5, 2, 8 * RANK, block), BF),
            pltpu.VMEM((5, 8 * RANK, block // 2), BF),
            pltpu.VMEM((5, 8 * RANK, block // 2), BF),
            pltpu.VMEM((2 * block, probes), F32),
            pltpu.VMEM((ups, 2, RANK, probes), BF),
            pltpu.SemaphoreType.DMA((CHUNKS,)),
            pltpu.SemaphoreType.DMA,
            pltpu.SemaphoreType.DMA((count, CHUNKS + 1)),
            pltpu.SemaphoreType.DMA((count, CHUNKS + 1)),
            pltpu.SemaphoreType.DMA((ups,)),
            pltpu.SemaphoreType.DMA((ups,)),
        ],
        compiler_params=pltpu.CompilerParams(
            collective_id=0, has_side_effects=True, vmem_limit_bytes=60 * 2**20),
    )(points, leaf_basis, side_by_side(local_transfer), side_by_side(top_transfer), keys, couplings)


def solution(mesh):
    placed = (
        P("leaf", "probe"),
        P("leaf", None, None),
        P("leaf", None),
        P(),
        P("leaf"),
        P("leaf", None),
    )
    return jax.shard_map(
        shards,
        mesh=mesh,
        in_specs=placed,
        out_specs=(P("leaf", None, "probe"), P("leaf", None, None, "probe")),
        check_vma=False,
    )
```

```python
import functools

import jax
import jax.numpy as jnp
import numpy as np
from jax import lax
from jax.experimental import pallas as pl
from jax.experimental.pallas import tpu as pltpu
from jax.sharding import PartitionSpec as P

RANK = 64
CHUNKS = 4
BF = jnp.bfloat16
F32 = jnp.float32


def matmul(a, b):
    return lax.dot_general(a, b, (((1,), (0,)), ((), ())), preferred_element_type=F32)


def matmul_t(a, b):
    return lax.dot_general(a, b, (((0,), (0,)), ((), ())), preferred_element_type=F32)


class Route:
    def __init__(self, sends, target, takes, origin, after):
        self.sends = sends
        self.target = target
        self.takes = takes
        self.origin = origin
        self.after = after


def routes_of(n, me):
    def among(*devices):
        found = me == devices[0]
        for device in devices[1:]:
            found = found | (me == device)
        return found

    if n == 8:
        flip = [me + 1 - 2 * (me % 2), me + 2 - 4 * ((me // 2) % 2), me + 4 - 8 * (me // 4)]
        other = 7 - me
        always = me >= 0
        cross3 = flip[1] + 1 - 2 * (flip[1] % 2)
        cross6 = flip[1] + 4 - 8 * (flip[1] // 4)
        return [
            Route(always, flip[0], always, flip[0], None),
            Route(always, flip[1], always, flip[1], None),
            Route(among(0, 3, 4, 7), flip[0], among(1, 2, 5, 6), cross3, 1),
            Route(among(0, 1, 6, 7), flip[2], among(2, 3, 4, 5), cross6, 1),
            Route(among(2, 5), flip[0], among(3, 4), other, 3),
        ]
    return [
        Route((me + o >= 0) & (me + o < n), me + o, (me - o >= 0) & (me - o < n), me - o, None)
        for o in (1, -1, 2, -2)
    ]


def kernel(n, leaves, probes, points, basis, lifts, tops, holders, couplings, coupled, ancestors,
           pts, tiles, own, got, got_lifts, lifted, spread, unrolled, square, w0, w1, wu, acc,
           ladder,
           pts_sem, tile_sem, send_sem, recv_sem, up_send, up_recv):
    me = lax.axis_index("leaf")
    ups = n.bit_length() - 1
    leaf = pts.shape[0] // leaves
    per = leaves // CHUNKS
    routes = routes_of(n, me)
    partners = []
    for h in range(ups):
        bit = (me // (1 << h)) % 2
        partners.append((bit, me + (1 << h) * (1 - 2 * bit)))

    def point_copy(k):
        rows = pl.ds(k * per * leaf, per * leaf)
        return pltpu.make_async_copy(points.at[rows, :], pts.at[rows, :], pts_sem.at[k])

    tile_copy = pltpu.make_async_copy(couplings, tiles, tile_sem)
    for k in range(CHUNKS):
        point_copy(k).start()
    tile_copy.start()

    barrier = pltpu.get_barrier_semaphore()
    greeted = [(None, device) for _, device in partners]
    if n != 8:
        greeted += [(r.sends, r.target) for r in routes]
    for valid, device in greeted:
        def greet(device=device):
            pl.semaphore_signal(barrier, inc=1, device_id={"leaf": device},
                                device_id_type=pl.DeviceIdType.MESH)
        greet() if valid is None else pl.when(valid)(greet)
    expected = ups
    if n != 8:
        expected += sum(r.takes.astype(jnp.int32) for r in routes)
    pl.semaphore_wait(barrier, expected)

    def move(i, k):
        route = routes[i]
        if k == CHUNKS:
            src = lifts if route.after is None else got_lifts.at[route.after]
            dst = got_lifts.at[i]
        else:
            rows = pl.ds(k * per * RANK, per * RANK)
            src = own.at[rows, :] if route.after is None else got.at[route.after, rows, :]
            dst = got.at[i, rows, :]
        return pltpu.make_async_remote_copy(
            src_ref=src, dst_ref=dst, send_sem=send_sem.at[i, k], recv_sem=recv_sem.at[i, k],
            device_id={"leaf": route.target}, device_id_type=pl.DeviceIdType.MESH)

    def send(i, k):
        pl.when(routes[i].sends)(lambda: move(i, k).start())

    arrived = set()

    def arrive(i, k):
        if (i, k) in arrived:
            return
        arrived.add((i, k))
        pl.when(routes[i].takes)(lambda: move(i, k).wait_recv())
        for later, route in enumerate(routes):
            if route.after == i:
                send(later, k)

    for i, route in enumerate(routes):
        if route.after is None:
            send(i, CHUNKS)

    for k in range(CHUNKS):
        point_copy(k).wait()
        for j in range(k * per, (k + 1) * per):
            own[j * RANK:(j + 1) * RANK, :] = matmul(
                basis[j], pts[j * leaf:(j + 1) * leaf, :]).astype(BF)
        for i, route in enumerate(routes):
            if route.after is None:
                send(i, k)

    def lift_all(source, matrices):
        half = leaves // 2
        for i in range(leaves - 1):
            if i < half:
                pair = source[2 * i * RANK:(2 * i + 2) * RANK, :]
            else:
                at = 2 * (i - half)
                pair = lifted[at * RANK:(at + 2) * RANK, :]
            lifted[i * RANK:(i + 1) * RANK, :] = matmul(
                matrices[i * RANK:(i + 1) * RANK, :], pair).astype(BF)

    def climb(h):
        bit, device = partners[h]
        return pltpu.make_async_remote_copy(
            src_ref=ladder.at[h, bit], dst_ref=ladder.at[h, bit], send_sem=up_send.at[h],
            recv_sem=up_recv.at[h], device_id={"leaf": device}, device_id_type=pl.DeviceIdType.MESH)

    def climb_end(h):
        climb(h).wait_recv()
        pairs = sum(n >> (g + 1) for g in range(h))
        row = (pairs + me // (1 << (h + 1))) * RANK
        matrix = tops[pl.ds(pl.multiple_of(row, RANK), RANK), :]
        both = ladder[h].reshape(2 * RANK, probes)
        value = matmul(matrix, both).astype(BF)
        ancestors[0, h] = value
        if h + 1 < ups:
            ladder[h + 1, partners[h + 1][0]] = value
            climb(h + 1).start()

    lift_all(own, lifts)
    root = lifted[(leaves - 2) * RANK:(leaves - 1) * RANK, :].astype(F32)
    for c in range(probes // 128):
        for side in range(2):
            spread[c, pl.ds(side, RANK // 2, stride=2), :] = root[
                side * 32:(side + 1) * 32, c * 128:(c + 1) * 128]
    ladder[0, partners[0][0]] = jnp.concatenate(
        [spread[c] for c in range(probes // 128)], axis=1).astype(BF)
    climb(0).start()

    tile_copy.wait()
    square[0] = jnp.zeros((32, 128), BF)

    def open_rows(start, count, turn):
        for q in range(32):
            part = tiles[pl.ds(start, count), q * 128:(q + 1) * 128].astype(F32)
            unrolled[pl.ds(q, count, stride=32), :] = turn(part)
        square[pl.ds(start + 1, count)] = unrolled[:count * 32, :].astype(BF).reshape(count, 32, 128)

    def open_group(group, turns):
        def turn(part):
            return jnp.concatenate(
                [pltpu.roll(part[u * 8:(u + 1) * 8], turns[u], 1) for u in range(2)], axis=0)
        open_rows(pl.multiple_of(group * 16, 16), 16, turn)

    e0, e1 = 6 * leaves, 3 * leaves

    def open0(group):
        amount = (group // 3) % 2 * 64
        open_group(group, (amount, amount))

    def open1(step):
        open_group(step + leaves * 3 * leaves // 16,
                   ((2 * step // 3) % 2 * 64, ((2 * step + 1) // 3) % 2 * 64))

    def open_upper():
        start = leaves * e1 + (leaves // 2) * (e1 // 2)
        for low in range(start, tiles.shape[0], 16):
            count = min(16, tiles.shape[0] - low)
            row = lax.broadcasted_iota(jnp.int32, (count, 128), 0) + (low - start)
            first = ((row < 12) | ((row >= 24) & (row < 36)) | ((row >= 48) & (row < 54))
                     | (row >= 60))
            open_rows(low, count, lambda part: jnp.where(first, part, pltpu.roll(part, 64, 1)))

    low_half = jnp.where(lax.broadcasted_iota(jnp.int32, (32, 128), 1) < 64, 1.0, 0.0)
    low_half = low_half.astype(BF) > BF(0.5)

    def place(weights, base, pair, slots):
        lanes = pl.ds(pl.multiple_of(pair * 128, 128), 128)
        for d in range(5):
            for s in range(slots):
                at = base + pair * 10 * slots + d * slots + s
                one = square[holders[at]]
                two = square[holders[at + 5 * slots]]
                rows = slice(s * 32, (s + 1) * 32)
                weights[d, 0, rows, lanes] = jnp.where(low_half, one, two)
                weights[d, 1, rows, lanes] = jnp.where(low_half, two, one)

    def halves(source, blocks):
        return [jnp.concatenate([source[s * RANK + side * 32:s * RANK + side * 32 + 32, :]
                                 for s in blocks], axis=0) for side in range(2)]

    def add_in(weights, columns, base, moments, fresh):
        @pl.loop(0, columns // 512)
        def _(c):
            at = pl.multiple_of(c * 512, 512)
            even = matmul_t(weights[0, :, pl.ds(at, 512)], moments[0])
            odd = matmul_t(weights[1, :, pl.ds(at, 512)], moments[1])
            for t in range(8):
                rows = pl.ds(pl.multiple_of(base + at + t * RANK, RANK), RANK)
                swap = t + 1 - 2 * (t % 2)
                part = even[t * RANK:(t + 1) * RANK] + odd[swap * RANK:(swap + 1) * RANK]
                if fresh:
                    acc[rows, :] = part
                else:
                    acc[rows, :] += part

    def couple(source, matrices, d, fresh=False, lift=True):
        if lift:
            lift_all(source, matrices)
        width = leaves * RANK
        add_in(w0.at[d], width, 0, halves(source, range(leaves)), fresh)
        add_in(w1.at[d], width // 2, width, halves(lifted, range(8)), fresh)
        add_in(wu.at[d], width // 2, width + width // 2,
               halves(lifted, (8, 9, 10, 11, 12, 13, 14, 14)), fresh)

    passed_on = sorted({r.after for r in routes if r.after is not None})
    for i in passed_on:
        arrive(i, CHUNKS)
    for step in range(4):
        pl.loop(12 * step, 12 * step + 12)(open0)
        if step < CHUNKS - 1:
            for i in passed_on:
                arrive(i, step)
        if step < ups:
            climb_end(step)
    for h in range(4, ups):
        climb_end(h)
    pl.loop(0, 12)(open1)
    open_upper()
    pl.loop(0, 8)(lambda j: place(w0, 0, j, 16))
    pl.loop(0, 4)(lambda j: place(w1, 1280, j, 8))
    pl.loop(0, 4)(lambda j: place(wu, 1600, j, 8))
    for i in passed_on:
        arrive(i, CHUNKS - 1)
    couple(own, lifts, 2, fresh=True, lift=False)
    for i, route in enumerate(routes):
        for k in range(CHUNKS + 1):
            arrive(i, k)

        @pl.when(route.takes)
        def _():
            couple(got.at[i], got_lifts.at[i], route.origin - me + 2)

    for t in range(2 * leaves - 1):
        coupled[t] = acc[t * RANK:(t + 1) * RANK, :].astype(BF)

    for i, route in enumerate(routes):
        for k in range(CHUNKS + 1):
            pl.when(route.sends)(lambda i=i, k=k: move(i, k).wait_send())
    for h in range(ups):
        climb(h).wait_send()


def side_by_side(matrices, halved):
    if halved:
        split = matrices.reshape(-1, 2, RANK // 2, 2, RANK // 2, 2)
        return split.transpose(0, 5, 4, 1, 3, 2).reshape(-1, 2 * RANK)
    return matrices.reshape(-1, 2, RANK, RANK).transpose(0, 3, 1, 2).reshape(-1, 2 * RANK)


def source_holders(sources, device, leaves):
    shifts, bases, widths = [], [], []
    for height in range(leaves.bit_length()):
        number = leaves >> height
        target = np.repeat(np.arange(number), 3 * number)
        if height == 0:
            bases.append(target * 5 * leaves)
        elif height == 1:
            bases.append(5 * leaves * leaves + target * 40)
        else:
            first = 8 - 2 * number
            bases.append(5 * leaves * leaves + 320 + (target + first) * 40 + first)
        shifts.append(np.full(3 * number * number, number.bit_length() - 1))
        widths.append(np.full(3 * number * number, leaves if height == 0 else 8))
    shift, base, width = (
        jnp.asarray(np.concatenate(x), jnp.int32) for x in (shifts, bases, widths))
    local = sources - ((device - 2) << shift)
    subtree = local >> shift
    key = base + subtree * width + local - (subtree << shift)
    slots = jnp.arange(5 * leaves * leaves + 640, dtype=jnp.int32)
    entry = jnp.arange(1, sources.shape[0] + 1, dtype=jnp.int32)
    return jnp.where(key[:, None] == slots[None, :], entry[:, None], 0).sum(axis=0)


def shards(points, leaf_basis, local_transfer, top_transfer, sources, couplings):
    n = lax.axis_size("leaf")
    leaves, _, leaf = leaf_basis.shape
    probes = points.shape[1]
    ups = n.bit_length() - 1
    holders = source_holders(sources, lax.axis_index("leaf"), leaves)
    halved_basis = leaf_basis.reshape(leaves, RANK // 2, 2, leaf).swapaxes(1, 2)
    halved_basis = halved_basis.reshape(leaves, RANK, leaf)
    block = leaves * RANK
    count = 5 if n == 8 else 4
    vmem = pl.BlockSpec(memory_space=pltpu.VMEM)
    anywhere = pl.BlockSpec(memory_space=pl.ANY)
    return pl.pallas_call(
        functools.partial(kernel, n, leaves, probes),
        out_shape=(
            jax.ShapeDtypeStruct((2 * leaves - 1, RANK, probes), BF),
            jax.ShapeDtypeStruct((1, ups, RANK, probes), BF),
        ),
        in_specs=[anywhere, vmem, vmem, vmem, pl.BlockSpec(memory_space=pltpu.SMEM), anywhere],
        out_specs=(vmem, vmem),
        scratch_shapes=[
            pltpu.VMEM(points.shape, BF),
            pltpu.VMEM(couplings.shape, BF),
            pltpu.VMEM((block, probes), BF),
            pltpu.VMEM((count, block, probes), BF),
            pltpu.VMEM((count, block - RANK, 2 * RANK), BF),
            pltpu.VMEM((block - RANK, probes), BF),
            pltpu.VMEM((probes // 128, RANK, 128), F32),
            pltpu.VMEM((16 * 32, 128), F32),
            pltpu.VMEM((couplings.shape[0] + 1, 32, 128), BF),
            pltpu.VMEM((5, 2, block // 2, block), BF),
            pltpu.VMEM((5, 2, block // 4, block // 2), BF),
            pltpu.VMEM((5, 2, block // 4, block // 2), BF),
            pltpu.VMEM((2 * block, probes), F32),
            pltpu.VMEM((ups, 2, RANK, probes), BF),
            pltpu.SemaphoreType.DMA((CHUNKS,)),
            pltpu.SemaphoreType.DMA,
            pltpu.SemaphoreType.DMA((count, CHUNKS + 1)),
            pltpu.SemaphoreType.DMA((count, CHUNKS + 1)),
            pltpu.SemaphoreType.DMA((ups,)),
            pltpu.SemaphoreType.DMA((ups,)),
        ],
        compiler_params=pltpu.CompilerParams(
            collective_id=0, has_side_effects=True, vmem_limit_bytes=60 * 2**20),
    )(points, halved_basis, side_by_side(local_transfer, True),
      side_by_side(top_transfer, False), holders, couplings)


def solution(mesh):
    placed = (
        P("leaf", "probe"),
        P("leaf", None, None),
        P("leaf", None),
        P(),
        P("leaf"),
        P("leaf", None),
    )
    return jax.shard_map(
        shards,
        mesh=mesh,
        in_specs=placed,
        out_specs=(P("leaf", None, "probe"), P("leaf", None, None, "probe")),
        check_vma=False,
    )
```

```python
import functools

import jax
import jax.numpy as jnp
import numpy as np
from jax import lax
from jax.experimental import pallas as pl
from jax.experimental.pallas import tpu as pltpu
from jax.sharding import PartitionSpec as P

RANK = 64
CHUNKS = 4
BF = jnp.bfloat16
F32 = jnp.float32


def matmul(a, b):
    return lax.dot_general(a, b, (((1,), (0,)), ((), ())), preferred_element_type=F32)


def matmul_t(a, b):
    return lax.dot_general(a, b, (((0,), (0,)), ((), ())), preferred_element_type=F32)


class Route:
    def __init__(self, sends, target, takes, origin, after):
        self.sends = sends
        self.target = target
        self.takes = takes
        self.origin = origin
        self.after = after


def routes_of(n, me):
    def among(*devices):
        found = me == devices[0]
        for device in devices[1:]:
            found = found | (me == device)
        return found

    if n == 8:
        flip = [me + 1 - 2 * (me % 2), me + 2 - 4 * ((me // 2) % 2), me + 4 - 8 * (me // 4)]
        other = 7 - me
        always = me >= 0
        cross3 = flip[1] + 1 - 2 * (flip[1] % 2)
        cross6 = flip[1] + 4 - 8 * (flip[1] // 4)
        return [
            Route(always, flip[0], always, flip[0], None),
            Route(always, flip[1], always, flip[1], None),
            Route(among(0, 3, 4, 7), flip[0], among(1, 2, 5, 6), cross3, 1),
            Route(among(0, 1, 6, 7), flip[2], among(2, 3, 4, 5), cross6, 1),
            Route(among(2, 5), flip[0], among(3, 4), other, 3),
        ]
    return [
        Route((me + o >= 0) & (me + o < n), me + o, (me - o >= 0) & (me - o < n), me - o, None)
        for o in (1, -1, 2, -2)
    ]


def kernel(n, leaves, probes, points, basis, whole_lifts, tops, holders, couplings, coupled, ancestors,
           pts, tiles, own, lifts, got, got_lifts, lifted, spread, unrolled, square, w0, w1, wu, acc,
           ladder,
           pts_sem, tile_sem, send_sem, recv_sem, up_send, up_recv):
    me = lax.axis_index("leaf")
    ups = n.bit_length() - 1
    leaf = pts.shape[0] // leaves
    per = leaves // CHUNKS
    routes = routes_of(n, me)
    partners = []
    for h in range(ups):
        bit = (me // (1 << h)) % 2
        partners.append((bit, me + (1 << h) * (1 - 2 * bit)))

    def point_copy(k):
        rows = pl.ds(k * per * leaf, per * leaf)
        return pltpu.make_async_copy(points.at[rows, :], pts.at[rows, :], pts_sem.at[k])

    tile_copy = pltpu.make_async_copy(couplings, tiles, tile_sem)
    for k in range(CHUNKS):
        point_copy(k).start()
    tile_copy.start()

    new = lax.broadcasted_iota(jnp.int32, (128, 128), 0)
    old = lax.broadcasted_iota(jnp.int32, (128, 128), 1)
    halve = jnp.where(old == new // 64 * 64 + new % 32 * 2 + new % 64 // 32, 1.0, 0.0).astype(BF)
    for at in range(0, whole_lifts.shape[0], 128):
        rows = min(128, whole_lifts.shape[0] - at)
        turned = matmul(halve[:rows, :rows], whole_lifts[at:at + rows, :]).astype(BF)
        lifts[at:at + rows, :] = lax.dot_general(
            turned, halve, (((1,), (1,)), ((), ())), preferred_element_type=F32).astype(BF)

    barrier = pltpu.get_barrier_semaphore()
    greeted = [(None, device) for _, device in partners]
    if n != 8:
        greeted += [(r.sends, r.target) for r in routes]
    for valid, device in greeted:
        def greet(device=device):
            pl.semaphore_signal(barrier, inc=1, device_id={"leaf": device},
                                device_id_type=pl.DeviceIdType.MESH)
        greet() if valid is None else pl.when(valid)(greet)
    expected = ups
    if n != 8:
        expected += sum(r.takes.astype(jnp.int32) for r in routes)
    pl.semaphore_wait(barrier, expected)

    def move(i, k):
        route = routes[i]
        if k == CHUNKS:
            src = lifts if route.after is None else got_lifts.at[route.after]
            dst = got_lifts.at[i]
        else:
            rows = pl.ds(k * per * RANK, per * RANK)
            src = own.at[rows, :] if route.after is None else got.at[route.after, rows, :]
            dst = got.at[i, rows, :]
        return pltpu.make_async_remote_copy(
            src_ref=src, dst_ref=dst, send_sem=send_sem.at[i, k], recv_sem=recv_sem.at[i, k],
            device_id={"leaf": route.target}, device_id_type=pl.DeviceIdType.MESH)

    def send(i, k):
        pl.when(routes[i].sends)(lambda: move(i, k).start())

    arrived = set()

    def arrive(i, k):
        if (i, k) in arrived:
            return
        arrived.add((i, k))
        pl.when(routes[i].takes)(lambda: move(i, k).wait_recv())
        for later, route in enumerate(routes):
            if route.after == i:
                send(later, k)

    for i, route in enumerate(routes):
        if route.after is None:
            send(i, CHUNKS)

    for k in range(CHUNKS):
        point_copy(k).wait()
        for j in range(k * per, (k + 1) * per):
            own[j * RANK:(j + 1) * RANK, :] = matmul(
                basis[j], pts[j * leaf:(j + 1) * leaf, :]).astype(BF)
        for i, route in enumerate(routes):
            if route.after is None:
                send(i, k)

    def lift_all(source, matrices):
        half = leaves // 2
        for i in range(leaves - 1):
            if i < half:
                pair = source[2 * i * RANK:(2 * i + 2) * RANK, :]
            else:
                at = 2 * (i - half)
                pair = lifted[at * RANK:(at + 2) * RANK, :]
            lifted[i * RANK:(i + 1) * RANK, :] = matmul(
                matrices[i * RANK:(i + 1) * RANK, :], pair).astype(BF)

    def climb(h):
        bit, device = partners[h]
        return pltpu.make_async_remote_copy(
            src_ref=ladder.at[h, bit], dst_ref=ladder.at[h, bit], send_sem=up_send.at[h],
            recv_sem=up_recv.at[h], device_id={"leaf": device}, device_id_type=pl.DeviceIdType.MESH)

    def climb_end(h):
        climb(h).wait_recv()
        pairs = sum(n >> (g + 1) for g in range(h))
        row = (pairs + me // (1 << (h + 1))) * RANK
        matrix = tops[pl.ds(pl.multiple_of(row, RANK), RANK), :]
        both = ladder[h].reshape(2 * RANK, probes)
        value = matmul(matrix, both).astype(BF)
        ancestors[0, h] = value
        if h + 1 < ups:
            ladder[h + 1, partners[h + 1][0]] = value
            climb(h + 1).start()

    lift_all(own, lifts)
    root = lifted[(leaves - 2) * RANK:(leaves - 1) * RANK, :].astype(F32)
    for c in range(probes // 128):
        for side in range(2):
            spread[c, pl.ds(side, RANK // 2, stride=2), :] = root[
                side * 32:(side + 1) * 32, c * 128:(c + 1) * 128]
    ladder[0, partners[0][0]] = jnp.concatenate(
        [spread[c] for c in range(probes // 128)], axis=1).astype(BF)
    climb(0).start()

    tile_copy.wait()
    square[0] = jnp.zeros((32, 128), BF)

    def open_rows(start, count, turn):
        for q in range(32):
            part = tiles[pl.ds(start, count), q * 128:(q + 1) * 128].astype(F32)
            unrolled[pl.ds(q, count, stride=32), :] = turn(part)
        square[pl.ds(start + 1, count)] = unrolled[:count * 32, :].astype(BF).reshape(count, 32, 128)

    out_row = lax.broadcasted_iota(jnp.int32, (256, 256), 0)
    in_row = lax.broadcasted_iota(jnp.int32, (256, 256), 1)
    regroup = jnp.where(in_row == out_row % 16 * 16 + out_row // 16, 1.0, 0.0).astype(BF)

    def open_two(left, right, turned):
        for half in range(2):
            stacked = jnp.concatenate([
                jnp.concatenate([tiles[pl.ds(at, 16), q * 128:(q + 1) * 128]
                                 for at in (left, right)], axis=1)
                for q in range(half * 16, half * 16 + 16)], axis=0)
            opened = matmul(regroup, stacked)
            for side, at in enumerate((left, right)):
                part = opened[:, side * 128:(side + 1) * 128]
                cut = turned[side] * 16
                if cut == 0:
                    part = pltpu.roll(part, 64, 1)
                elif cut < 256:
                    part = jnp.concatenate([part[:cut], pltpu.roll(part[cut:], 64, 1)], axis=0)
                square[pl.ds(at + 1, 16), half * 16:half * 16 + 16, :] = (
                    part.astype(BF).reshape(16, 16, 128))

    e0, e1 = 6 * leaves, 3 * leaves

    def open0(pair):
        for u in range(e0 // 32):
            left = pl.multiple_of(pair * e0 + u * 16, 16)
            open_two(left, pl.multiple_of(left + e0 // 2, 16), (16, 0))

    def open1(step):
        at = pl.multiple_of(leaves * e1 + step * 2 * e1, 16)
        open_two(at, pl.multiple_of(at + 32, 16), (16, 0))
        open_two(pl.multiple_of(at + 48, 16), pl.multiple_of(at + 80, 16), (16, 0))
        open_two(pl.multiple_of(at + 16, 16), pl.multiple_of(at + 64, 16), (8, 8))

    def open_upper():
        start = leaves * e1 + (leaves // 2) * (e1 // 2)
        for low in range(start, tiles.shape[0], 16):
            count = min(16, tiles.shape[0] - low)
            row = lax.broadcasted_iota(jnp.int32, (count, 128), 0) + (low - start)
            first = ((row < 12) | ((row >= 24) & (row < 36)) | ((row >= 48) & (row < 54))
                     | (row >= 60))
            open_rows(low, count, lambda part: jnp.where(first, part, pltpu.roll(part, 64, 1)))

    low_half = jnp.where(lax.broadcasted_iota(jnp.int32, (32, 128), 1) < 64, 1.0, 0.0)
    low_half = low_half.astype(BF) > BF(0.5)

    def place(weights, base, pair, slots):
        lanes = pl.ds(pl.multiple_of(pair * 128, 128), 128)
        for d in range(5):
            for s in range(slots):
                at = base + pair * 10 * slots + d * slots + s
                one = square[holders[at]]
                two = square[holders[at + 5 * slots]]
                rows = slice(s * 32, (s + 1) * 32)
                weights[d, 0, rows, lanes] = jnp.where(low_half, one, two)
                weights[d, 1, rows, lanes] = jnp.where(low_half, two, one)

    def halves(source, blocks):
        return [jnp.concatenate([source[s * RANK + side * 32:s * RANK + side * 32 + 32, :]
                                 for s in blocks], axis=0) for side in range(2)]

    def add_in(weights, columns, base, moments, fresh):
        @pl.loop(0, columns // 512)
        def _(c):
            at = pl.multiple_of(c * 512, 512)
            even = matmul_t(weights[0, :, pl.ds(at, 512)], moments[0])
            odd = matmul_t(weights[1, :, pl.ds(at, 512)], moments[1])
            for t in range(8):
                rows = pl.ds(pl.multiple_of(base + at + t * RANK, RANK), RANK)
                swap = t + 1 - 2 * (t % 2)
                part = even[t * RANK:(t + 1) * RANK] + odd[swap * RANK:(swap + 1) * RANK]
                if fresh:
                    acc[rows, :] = part
                else:
                    acc[rows, :] += part

    def couple(source, matrices, d, fresh=False, lift=True):
        if lift:
            lift_all(source, matrices)
        width = leaves * RANK
        add_in(w0.at[d], width, 0, halves(source, range(leaves)), fresh)
        add_in(w1.at[d], width // 2, width, halves(lifted, range(8)), fresh)
        add_in(wu.at[d], width // 2, width + width // 2,
               halves(lifted, (8, 9, 10, 11, 12, 13, 14, 14)), fresh)

    passed_on = sorted({r.after for r in routes if r.after is not None})
    for i in passed_on:
        arrive(i, CHUNKS)
    for step in range(4):
        pl.loop(2 * step, 2 * step + 2)(open0)
        if step < CHUNKS - 1:
            for i in passed_on:
                arrive(i, step)
        if step < ups:
            climb_end(step)
    for h in range(4, ups):
        climb_end(h)
    pl.loop(0, 2)(open1)
    open_upper()
    pl.loop(0, 8)(lambda j: place(w0, 0, j, 16))
    pl.loop(0, 4)(lambda j: place(w1, 1280, j, 8))
    pl.loop(0, 4)(lambda j: place(wu, 1600, j, 8))
    for i in passed_on:
        arrive(i, CHUNKS - 1)
    couple(own, lifts, 2, fresh=True, lift=False)
    for i, route in enumerate(routes):
        for k in range(CHUNKS + 1):
            arrive(i, k)

        @pl.when(route.takes)
        def _():
            couple(got.at[i], got_lifts.at[i], route.origin - me + 2)

    for t in range(2 * leaves - 1):
        coupled[t] = acc[t * RANK:(t + 1) * RANK, :].astype(BF)

    for i, route in enumerate(routes):
        for k in range(CHUNKS + 1):
            pl.when(route.sends)(lambda i=i, k=k: move(i, k).wait_send())
    for h in range(ups):
        climb(h).wait_send()


def side_by_side(matrices):
    return matrices.reshape(-1, 2, RANK, RANK).transpose(0, 3, 1, 2).reshape(-1, 2 * RANK)


def source_holders(sources, device, leaves):
    shifts, bases, widths = [], [], []
    for height in range(leaves.bit_length()):
        number = leaves >> height
        target = np.repeat(np.arange(number), 3 * number)
        if height == 0:
            bases.append(target * 5 * leaves)
        elif height == 1:
            bases.append(5 * leaves * leaves + target * 40)
        else:
            first = 8 - 2 * number
            bases.append(5 * leaves * leaves + 320 + (target + first) * 40 + first)
        shifts.append(np.full(3 * number * number, number.bit_length() - 1))
        widths.append(np.full(3 * number * number, leaves if height == 0 else 8))
    shift, base, width = (
        jnp.asarray(np.concatenate(x), jnp.int32) for x in (shifts, bases, widths))
    local = sources - ((device - 2) << shift)
    subtree = local >> shift
    key = base + subtree * width + local - (subtree << shift)
    slots = jnp.arange(5 * leaves * leaves + 640, dtype=jnp.int32)
    entry = jnp.arange(1, sources.shape[0] + 1, dtype=jnp.int32)
    return jnp.where(key[:, None] == slots[None, :], entry[:, None], 0).sum(axis=0)


def shards(points, leaf_basis, local_transfer, top_transfer, sources, couplings):
    n = lax.axis_size("leaf")
    leaves, _, leaf = leaf_basis.shape
    probes = points.shape[1]
    ups = n.bit_length() - 1
    holders = source_holders(sources, lax.axis_index("leaf"), leaves)
    halved_basis = leaf_basis.reshape(leaves, RANK // 2, 2, leaf).swapaxes(1, 2)
    halved_basis = halved_basis.reshape(leaves, RANK, leaf)
    block = leaves * RANK
    count = 5 if n == 8 else 4
    vmem = pl.BlockSpec(memory_space=pltpu.VMEM)
    anywhere = pl.BlockSpec(memory_space=pl.ANY)
    return pl.pallas_call(
        functools.partial(kernel, n, leaves, probes),
        out_shape=(
            jax.ShapeDtypeStruct((2 * leaves - 1, RANK, probes), BF),
            jax.ShapeDtypeStruct((1, ups, RANK, probes), BF),
        ),
        in_specs=[anywhere, vmem, vmem, vmem, pl.BlockSpec(memory_space=pltpu.SMEM), anywhere],
        out_specs=(vmem, vmem),
        scratch_shapes=[
            pltpu.VMEM(points.shape, BF),
            pltpu.VMEM(couplings.shape, BF),
            pltpu.VMEM((block, probes), BF),
            pltpu.VMEM((block - RANK, 2 * RANK), BF),
            pltpu.VMEM((count, block, probes), BF),
            pltpu.VMEM((count, block - RANK, 2 * RANK), BF),
            pltpu.VMEM((block - RANK, probes), BF),
            pltpu.VMEM((probes // 128, RANK, 128), F32),
            pltpu.VMEM((16 * 32, 128), F32),
            pltpu.VMEM((couplings.shape[0] + 1, 32, 128), BF),
            pltpu.VMEM((5, 2, block // 2, block), BF),
            pltpu.VMEM((5, 2, block // 4, block // 2), BF),
            pltpu.VMEM((5, 2, block // 4, block // 2), BF),
            pltpu.VMEM((2 * block, probes), F32),
            pltpu.VMEM((ups, 2, RANK, probes), BF),
            pltpu.SemaphoreType.DMA((CHUNKS,)),
            pltpu.SemaphoreType.DMA,
            pltpu.SemaphoreType.DMA((count, CHUNKS + 1)),
            pltpu.SemaphoreType.DMA((count, CHUNKS + 1)),
            pltpu.SemaphoreType.DMA((ups,)),
            pltpu.SemaphoreType.DMA((ups,)),
        ],
        compiler_params=pltpu.CompilerParams(
            collective_id=0, has_side_effects=True, vmem_limit_bytes=60 * 2**20),
    )(points, halved_basis, side_by_side(local_transfer),
      side_by_side(top_transfer), holders, couplings)


def solution(mesh):
    placed = (
        P("leaf", "probe"),
        P("leaf", None, None),
        P("leaf", None),
        P(),
        P("leaf"),
        P("leaf", None),
    )
    return jax.shard_map(
        shards,
        mesh=mesh,
        in_specs=placed,
        out_specs=(P("leaf", None, "probe"), P("leaf", None, None, "probe")),
        check_vma=False,
    )
```

```python
import functools

import jax
import jax.numpy as jnp
import numpy as np
from jax import lax
from jax.experimental import pallas as pl
from jax.experimental.pallas import tpu as pltpu
from jax.sharding import PartitionSpec as P

RANK = 64
CHUNKS = 4
BF = jnp.bfloat16
F32 = jnp.float32


def matmul(a, b):
    return lax.dot_general(a, b, (((1,), (0,)), ((), ())), preferred_element_type=F32)


def matmul_t(a, b):
    return lax.dot_general(a, b, (((0,), (0,)), ((), ())), preferred_element_type=F32)


class Route:
    def __init__(self, sends, target, takes, origin, after):
        self.sends = sends
        self.target = target
        self.takes = takes
        self.origin = origin
        self.after = after


def routes_of(n, me):
    def among(*devices):
        found = me == devices[0]
        for device in devices[1:]:
            found = found | (me == device)
        return found

    if n == 8:
        flip = [me + 1 - 2 * (me % 2), me + 2 - 4 * ((me // 2) % 2), me + 4 - 8 * (me // 4)]
        other = 7 - me
        always = me >= 0
        cross3 = flip[1] + 1 - 2 * (flip[1] % 2)
        cross6 = flip[1] + 4 - 8 * (flip[1] // 4)
        return [
            Route(always, flip[0], always, flip[0], None),
            Route(always, flip[1], always, flip[1], None),
            Route(among(0, 3, 4, 7), flip[0], among(1, 2, 5, 6), cross3, 1),
            Route(among(0, 1, 6, 7), flip[2], among(2, 3, 4, 5), cross6, 1),
            Route(among(2, 5), flip[0], among(3, 4), other, 3),
        ]
    return [
        Route((me + o >= 0) & (me + o < n), me + o, (me - o >= 0) & (me - o < n), me - o, None)
        for o in (1, -1, 2, -2)
    ]


def kernel(n, leaves, probes, points, whole_basis, matrices, holders, couplings, coupled, ancestors,
           pts, tiles, basis, own, lifts, got, got_lifts, lifted, spread, unrolled, square, w0, w1, wu, acc,
           ladder,
           pts_sem, tile_sem, send_sem, recv_sem, up_send, up_recv):
    me = lax.axis_index("leaf")
    ups = n.bit_length() - 1
    leaf = pts.shape[0] // leaves
    per = leaves // CHUNKS
    routes = routes_of(n, me)
    partners = []
    for h in range(ups):
        bit = (me // (1 << h)) % 2
        partners.append((bit, me + (1 << h) * (1 - 2 * bit)))

    def point_copy(k):
        rows = pl.ds(k * per * leaf, per * leaf)
        return pltpu.make_async_copy(points.at[rows, :], pts.at[rows, :], pts_sem.at[k])

    tile_copy = pltpu.make_async_copy(couplings, tiles, tile_sem)
    for k in range(CHUNKS):
        point_copy(k).start()
    tile_copy.start()

    new = lax.broadcasted_iota(jnp.int32, (128, 128), 0)
    old = lax.broadcasted_iota(jnp.int32, (128, 128), 1)
    halve = jnp.where(old == new // 64 * 64 + new % 32 * 2 + new % 64 // 32, 1.0, 0.0).astype(BF)
    for j in range(leaves):
        basis[j] = matmul(halve[:RANK, :RANK], whole_basis[j]).astype(BF)
    for at in range(0, lifts.shape[0], 128):
        rows = min(128, lifts.shape[0] - at)
        turned = matmul(halve[:rows, :rows], matrices[at:at + rows, :]).astype(BF)
        lifts[at:at + rows, :] = lax.dot_general(
            turned, halve, (((1,), (1,)), ((), ())), preferred_element_type=F32).astype(BF)

    barrier = pltpu.get_barrier_semaphore()
    greeted = [(None, device) for _, device in partners]
    if n != 8:
        greeted += [(r.sends, r.target) for r in routes]
    for valid, device in greeted:
        def greet(device=device):
            pl.semaphore_signal(barrier, inc=1, device_id={"leaf": device},
                                device_id_type=pl.DeviceIdType.MESH)
        greet() if valid is None else pl.when(valid)(greet)
    expected = ups
    if n != 8:
        expected += sum(r.takes.astype(jnp.int32) for r in routes)
    pl.semaphore_wait(barrier, expected)

    def move(i, k):
        route = routes[i]
        if k == CHUNKS:
            src = lifts if route.after is None else got_lifts.at[route.after]
            dst = got_lifts.at[i]
        else:
            rows = pl.ds(k * per * RANK, per * RANK)
            src = own.at[rows, :] if route.after is None else got.at[route.after, rows, :]
            dst = got.at[i, rows, :]
        return pltpu.make_async_remote_copy(
            src_ref=src, dst_ref=dst, send_sem=send_sem.at[i, k], recv_sem=recv_sem.at[i, k],
            device_id={"leaf": route.target}, device_id_type=pl.DeviceIdType.MESH)

    def send(i, k):
        pl.when(routes[i].sends)(lambda: move(i, k).start())

    arrived = set()

    def arrive(i, k):
        if (i, k) in arrived:
            return
        arrived.add((i, k))
        pl.when(routes[i].takes)(lambda: move(i, k).wait_recv())
        for later, route in enumerate(routes):
            if route.after == i:
                send(later, k)

    for i, route in enumerate(routes):
        if route.after is None:
            send(i, CHUNKS)

    for k in range(CHUNKS):
        point_copy(k).wait()
        for j in range(k * per, (k + 1) * per):
            own[j * RANK:(j + 1) * RANK, :] = matmul(
                basis[j], pts[j * leaf:(j + 1) * leaf, :]).astype(BF)
        for i, route in enumerate(routes):
            if route.after is None:
                send(i, k)

    def lift_all(source, matrices):
        half = leaves // 2
        for i in range(leaves - 1):
            if i < half:
                pair = source[2 * i * RANK:(2 * i + 2) * RANK, :]
            else:
                at = 2 * (i - half)
                pair = lifted[at * RANK:(at + 2) * RANK, :]
            lifted[i * RANK:(i + 1) * RANK, :] = matmul(
                matrices[i * RANK:(i + 1) * RANK, :], pair).astype(BF)

    def climb(h):
        bit, device = partners[h]
        return pltpu.make_async_remote_copy(
            src_ref=ladder.at[h, bit], dst_ref=ladder.at[h, bit], send_sem=up_send.at[h],
            recv_sem=up_recv.at[h], device_id={"leaf": device}, device_id_type=pl.DeviceIdType.MESH)

    def climb_end(h):
        climb(h).wait_recv()
        pairs = sum(n >> (g + 1) for g in range(h))
        row = (leaves - 1 + pairs + me // (1 << (h + 1))) * RANK
        matrix = matrices[pl.ds(pl.multiple_of(row, RANK), RANK), :]
        both = ladder[h].reshape(2 * RANK, probes)
        value = matmul(matrix, both).astype(BF)
        ancestors[0, h] = value
        if h + 1 < ups:
            ladder[h + 1, partners[h + 1][0]] = value
            climb(h + 1).start()

    lift_all(own, lifts)
    root = lifted[(leaves - 2) * RANK:(leaves - 1) * RANK, :].astype(F32)
    for c in range(probes // 128):
        for side in range(2):
            spread[c, pl.ds(side, RANK // 2, stride=2), :] = root[
                side * 32:(side + 1) * 32, c * 128:(c + 1) * 128]
    ladder[0, partners[0][0]] = jnp.concatenate(
        [spread[c] for c in range(probes // 128)], axis=1).astype(BF)
    climb(0).start()

    tile_copy.wait()
    square[0] = jnp.zeros((32, 128), BF)

    def open_rows(start, count, turn):
        for q in range(32):
            part = tiles[pl.ds(start, count), q * 128:(q + 1) * 128].astype(F32)
            unrolled[pl.ds(q, count, stride=32), :] = turn(part)
        square[pl.ds(start + 1, count)] = unrolled[:count * 32, :].astype(BF).reshape(count, 32, 128)

    out_row = lax.broadcasted_iota(jnp.int32, (256, 256), 0)
    in_row = lax.broadcasted_iota(jnp.int32, (256, 256), 1)
    regroup = jnp.where(in_row == out_row % 16 * 16 + out_row // 16, 1.0, 0.0).astype(BF)

    def open_two(left, right, turned):
        for half in range(2):
            stacked = jnp.concatenate([
                jnp.concatenate([tiles[pl.ds(at, 16), q * 128:(q + 1) * 128]
                                 for at in (left, right)], axis=1)
                for q in range(half * 16, half * 16 + 16)], axis=0)
            opened = matmul(regroup, stacked)
            for side, at in enumerate((left, right)):
                part = opened[:, side * 128:(side + 1) * 128]
                cut = turned[side] * 16
                if cut == 0:
                    part = pltpu.roll(part, 64, 1)
                elif cut < 256:
                    part = jnp.concatenate([part[:cut], pltpu.roll(part[cut:], 64, 1)], axis=0)
                square[pl.ds(at + 1, 16), half * 16:half * 16 + 16, :] = (
                    part.astype(BF).reshape(16, 16, 128))

    e0, e1 = 6 * leaves, 3 * leaves

    def open0(pair):
        for u in range(e0 // 32):
            left = pl.multiple_of(pair * e0 + u * 16, 16)
            open_two(left, pl.multiple_of(left + e0 // 2, 16), (16, 0))

    def open1(step):
        at = pl.multiple_of(leaves * e1 + step * 2 * e1, 16)
        open_two(at, pl.multiple_of(at + 32, 16), (16, 0))
        open_two(pl.multiple_of(at + 48, 16), pl.multiple_of(at + 80, 16), (16, 0))
        open_two(pl.multiple_of(at + 16, 16), pl.multiple_of(at + 64, 16), (8, 8))

    def open_upper():
        start = leaves * e1 + (leaves // 2) * (e1 // 2)
        for low in range(start, tiles.shape[0], 16):
            count = min(16, tiles.shape[0] - low)
            row = lax.broadcasted_iota(jnp.int32, (count, 128), 0) + (low - start)
            first = ((row < 12) | ((row >= 24) & (row < 36)) | ((row >= 48) & (row < 54))
                     | (row >= 60))
            open_rows(low, count, lambda part: jnp.where(first, part, pltpu.roll(part, 64, 1)))

    low_half = jnp.where(lax.broadcasted_iota(jnp.int32, (32, 128), 1) < 64, 1.0, 0.0)
    low_half = low_half.astype(BF) > BF(0.5)

    def place(weights, base, pair, slots):
        lanes = pl.ds(pl.multiple_of(pair * 128, 128), 128)
        for d in range(5):
            for s in range(slots):
                at = base + pair * 10 * slots + d * slots + s
                one = square[holders[at]]
                two = square[holders[at + 5 * slots]]
                rows = slice(s * 32, (s + 1) * 32)
                weights[d, 0, rows, lanes] = jnp.where(low_half, one, two)
                weights[d, 1, rows, lanes] = jnp.where(low_half, two, one)

    def halves(source, blocks):
        return [jnp.concatenate([source[s * RANK + side * 32:s * RANK + side * 32 + 32, :]
                                 for s in blocks], axis=0) for side in range(2)]

    def add_in(weights, columns, base, moments, fresh):
        @pl.loop(0, columns // 512)
        def _(c):
            at = pl.multiple_of(c * 512, 512)
            even = matmul_t(weights[0, :, pl.ds(at, 512)], moments[0])
            odd = matmul_t(weights[1, :, pl.ds(at, 512)], moments[1])
            for t in range(8):
                rows = pl.ds(pl.multiple_of(base + at + t * RANK, RANK), RANK)
                swap = t + 1 - 2 * (t % 2)
                part = even[t * RANK:(t + 1) * RANK] + odd[swap * RANK:(swap + 1) * RANK]
                if fresh:
                    acc[rows, :] = part
                else:
                    acc[rows, :] += part

    def couple(source, matrices, d, fresh=False, lift=True):
        if lift:
            lift_all(source, matrices)
        width = leaves * RANK
        add_in(w0.at[d], width, 0, halves(source, range(leaves)), fresh)
        add_in(w1.at[d], width // 2, width, halves(lifted, range(8)), fresh)
        add_in(wu.at[d], width // 2, width + width // 2,
               halves(lifted, (8, 9, 10, 11, 12, 13, 14, 14)), fresh)

    passed_on = sorted({r.after for r in routes if r.after is not None})
    for i in passed_on:
        arrive(i, CHUNKS)
    for step in range(4):
        pl.loop(2 * step, 2 * step + 2)(open0)
        if step < CHUNKS - 1:
            for i in passed_on:
                arrive(i, step)
        if step < ups:
            climb_end(step)
    for h in range(4, ups):
        climb_end(h)
    pl.loop(0, 2)(open1)
    open_upper()
    pl.loop(0, 8)(lambda j: place(w0, 0, j, 16))
    pl.loop(0, 4)(lambda j: place(w1, 1280, j, 8))
    pl.loop(0, 4)(lambda j: place(wu, 1600, j, 8))
    for i in passed_on:
        arrive(i, CHUNKS - 1)
    couple(own, lifts, 2, fresh=True, lift=False)
    for i, route in enumerate(routes):
        for k in range(CHUNKS + 1):
            arrive(i, k)

        @pl.when(route.takes)
        def _():
            couple(got.at[i], got_lifts.at[i], route.origin - me + 2)

    for t in range(2 * leaves - 1):
        coupled[t] = acc[t * RANK:(t + 1) * RANK, :].astype(BF)

    for i, route in enumerate(routes):
        for k in range(CHUNKS + 1):
            pl.when(route.sends)(lambda i=i, k=k: move(i, k).wait_send())
    for h in range(ups):
        climb(h).wait_send()


def side_by_side(matrices):
    return matrices.reshape(-1, 2, RANK, RANK).transpose(0, 3, 1, 2).reshape(-1, 2 * RANK)


def source_holders(sources, device, leaves):
    shifts, bases, widths = [], [], []
    for height in range(leaves.bit_length()):
        number = leaves >> height
        target = np.repeat(np.arange(number), 3 * number)
        if height == 0:
            bases.append(target * 5 * leaves)
        elif height == 1:
            bases.append(5 * leaves * leaves + target * 40)
        else:
            first = 8 - 2 * number
            bases.append(5 * leaves * leaves + 320 + (target + first) * 40 + first)
        shifts.append(np.full(3 * number * number, number.bit_length() - 1))
        widths.append(np.full(3 * number * number, leaves if height == 0 else 8))
    shift, base, width = (
        jnp.asarray(np.concatenate(x), jnp.int32) for x in (shifts, bases, widths))
    local = sources - ((device - 2) << shift)
    subtree = local >> shift
    key = base + subtree * width + local - (subtree << shift)
    slots = jnp.arange(5 * leaves * leaves + 640, dtype=jnp.int32)
    entry = jnp.arange(1, sources.shape[0] + 1, dtype=jnp.int32)
    return jnp.where(key[:, None] == slots[None, :], entry[:, None], 0).sum(axis=0)


def shards(points, leaf_basis, local_transfer, top_transfer, sources, couplings):
    n = lax.axis_size("leaf")
    leaves = leaf_basis.shape[0]
    probes = points.shape[1]
    ups = n.bit_length() - 1
    holders = source_holders(sources, lax.axis_index("leaf"), leaves)
    block = leaves * RANK
    count = 5 if n == 8 else 4
    vmem = pl.BlockSpec(memory_space=pltpu.VMEM)
    anywhere = pl.BlockSpec(memory_space=pl.ANY)
    return pl.pallas_call(
        functools.partial(kernel, n, leaves, probes),
        out_shape=(
            jax.ShapeDtypeStruct((2 * leaves - 1, RANK, probes), BF),
            jax.ShapeDtypeStruct((1, ups, RANK, probes), BF),
        ),
        in_specs=[anywhere, vmem, vmem, pl.BlockSpec(memory_space=pltpu.SMEM), anywhere],
        out_specs=(vmem, vmem),
        scratch_shapes=[
            pltpu.VMEM(points.shape, BF),
            pltpu.VMEM(couplings.shape, BF),
            pltpu.VMEM(leaf_basis.shape, BF),
            pltpu.VMEM((block, probes), BF),
            pltpu.VMEM((block - RANK, 2 * RANK), BF),
            pltpu.VMEM((count, block, probes), BF),
            pltpu.VMEM((count, block - RANK, 2 * RANK), BF),
            pltpu.VMEM((block - RANK, probes), BF),
            pltpu.VMEM((probes // 128, RANK, 128), F32),
            pltpu.VMEM((16 * 32, 128), F32),
            pltpu.VMEM((couplings.shape[0] + 1, 32, 128), BF),
            pltpu.VMEM((5, 2, block // 2, block), BF),
            pltpu.VMEM((5, 2, block // 4, block // 2), BF),
            pltpu.VMEM((5, 2, block // 4, block // 2), BF),
            pltpu.VMEM((2 * block, probes), F32),
            pltpu.VMEM((ups, 2, RANK, probes), BF),
            pltpu.SemaphoreType.DMA((CHUNKS,)),
            pltpu.SemaphoreType.DMA,
            pltpu.SemaphoreType.DMA((count, CHUNKS + 1)),
            pltpu.SemaphoreType.DMA((count, CHUNKS + 1)),
            pltpu.SemaphoreType.DMA((ups,)),
            pltpu.SemaphoreType.DMA((ups,)),
        ],
        compiler_params=pltpu.CompilerParams(
            collective_id=0, has_side_effects=True, vmem_limit_bytes=60 * 2**20),
    )(points, leaf_basis, side_by_side(jnp.concatenate([local_transfer, top_transfer])),
      holders, couplings)


def solution(mesh):
    placed = (
        P("leaf", "probe"),
        P("leaf", None, None),
        P("leaf", None),
        P(),
        P("leaf"),
        P("leaf", None),
    )
    return jax.shard_map(
        shards,
        mesh=mesh,
        in_specs=placed,
        out_specs=(P("leaf", None, "probe"), P("leaf", None, None, "probe")),
        check_vma=False,
    )
```
